512 devices in a mesh: row: 16 (over z), col: 4 (over y), depth: 8 (over x, core).
Axes of the slice: x: 4, y: 4, z: 16, core: 2. Of those that a mesh axis runs over, the one named last changes fastest.
Arguments:
- left_block: bfloat16 [6144, 6144], P('row', 'col'), may hold values from -6 to 6
- right_block: bfloat16 [6144, 12288], P('row', 'col'), may hold values from -0.078125 to 0.078125
Outputs:
- block_product: float32 [6144, 12288], P('row', ('col', 'depth'))
The draws below stay inside these ranges and needn't reach their ends.
All inputs are finite; a program needn't handle non-finite values.
Results may differ from the reference program's by a relative error of at most 0.0003.
Values may be sent and summed in bfloat16 or wider, within the bound.
A program may use at most 64 MiB of HBM per device.

```python
import jax
import jax.numpy as jnp

M = 6144
K = 6144
N = 12288


def block_levels(rng, extent, shards, low, largest):
    gain = 1.0
    for axis_at, blocks in shards:
        heights = jax.random.uniform(jax.random.fold_in(jax.random.fold_in(rng, 6), axis_at), (blocks,), jnp.float32, low / len(shards), largest / len(shards))
        gain = gain * jnp.repeat(jnp.exp(heights), extent[axis_at] // blocks).reshape((-1,) + (1,) * (len(extent) - 1 - axis_at))
    return gain


def bell_draw(rng, dims, deviation, bound, shards=(), held_as=jnp.bfloat16):
    values = deviation * jax.random.normal(rng, dims, jnp.float32)
    if shards:
        values = values * block_levels(rng, dims, shards, -0.22, 0.18)
    return jnp.clip(values, -bound, bound).astype(held_as)


def setup_inputs(seed: int = 0) -> dict:
    key_of = jax.random.split(jax.random.key(seed), 3)
    left_block = bell_draw(key_of[0], (M, K), 1.0, 6.0, ((0, 16), (1, 4)))
    right_block = bell_draw(key_of[1], (K, N), K ** -0.5, 0.078125, ((0, 16), (1, 4)))
    return {"left_block": left_block, "right_block": right_block}


def reference(left_block, right_block):
    return jnp.dot(left_block, right_block, preferred_element_type=jnp.float32)
```

```python
import functools

import jax
import jax.numpy as jnp
from jax import lax
from jax.experimental import pallas as pl
from jax.experimental.pallas import tpu as pltpu
from jax.sharding import PartitionSpec as P

PIECES = 4
LEFT_NEAR = 3
LEFT_FAR = 4
LEFT_READY = 5


def kernel(
    left, right, out, lpan, rpan,
    own_sem, up_s, up_r, dn_s, dn_r, ly_s, ly_r, lc_s, lc_r,
):
    rows = lax.axis_size("row")
    cols = lax.axis_size("col")
    z, y, d = lax.axis_index("row"), lax.axis_index("col"), lax.axis_index("depth")
    depth, width = rpan.shape[1:]
    height = left.shape[0]
    half_steps = rows // 2
    piece = depth // PIECES
    per_col = left.shape[1] // depth

    z_up, z_dn = lax.rem(z + 1, rows), lax.rem(z + rows - 1, rows)
    y_up, y_dn = lax.rem(y + 1, cols), lax.rem(y + cols - 1, cols)
    y_far = lax.rem(y + 2, cols)
    core = lax.rem(d, 2)
    twin = d + 1 - 2 * core

    barrier = pltpu.get_barrier_semaphore()
    for who in ((z_up, y, d), (z_dn, y, d), (z, y_up, d), (z, y_dn, d), (z, y, twin)):
        pl.semaphore_signal(barrier, inc=1, device_id=who)
    pl.semaphore_wait(barrier, 5)

    my_cols = pl.ds(pl.multiple_of(d * width, 128), width)

    def up_rows(i):
        return pl.ds(i * piece, piece)

    def dn_rows(i):
        return pl.ds((i + PIECES // 2) % PIECES * piece, piece)

    def send(src, dst, send_sem, recv_sem, who):
        return pltpu.make_async_remote_copy(
            src_ref=src, dst_ref=dst, send_sem=send_sem, recv_sem=recv_sem,
            device_id=who,
        )

    def up_copy(step, i, first=False):
        chunk = lax.rem(z - step + 1 + rows, rows)
        dst = rpan.at[chunk, up_rows(i)]
        src = right.at[up_rows(i), my_cols] if first else dst
        return send(src, dst, up_s.at[step, i], up_r.at[step, i], (z_up, y, d))

    def dn_copy(step, i, first=False):
        chunk = lax.rem(z + step - 1, rows)
        dst = rpan.at[chunk, dn_rows(i)]
        src = right.at[dn_rows(i), my_cols] if first else dst
        return send(src, dst, dn_s.at[step, i], dn_r.at[step, i], (z_dn, y, d))

    def up_arrival(step, i):
        dst = rpan.at[lax.rem(z - step + rows, rows), up_rows(i)]
        return send(dst, dst, up_s.at[step, i], up_r.at[step, i], (z_up, y, d))

    def dn_arrival(step, i):
        dst = rpan.at[lax.rem(z + step, rows), dn_rows(i)]
        return send(dst, dst, dn_s.at[step, i], dn_r.at[step, i], (z_dn, y, d))

    for i in range(PIECES):
        up_copy(1, i, True).start()
        dn_copy(1, i, True).start()

    share = height // 2
    my_share = pl.ds(pl.multiple_of(core * share, 16), share)
    twin_share = pl.ds(pl.multiple_of((1 - core) * share, 16), share)
    first_part = pl.ds(pl.multiple_of(core * share, 16), share // 2)
    second_part = pl.ds(pl.multiple_of(core * share + share // 2, 16), share // 2)

    def near_copies():
        src, dst = left.at[my_share], lpan.at[y, my_share]
        return (
            send(src, dst, ly_s.at[0], ly_r.at[0], (z, y_up, d)),
            send(src, dst, ly_s.at[1], ly_r.at[1], (z, y_dn, d)),
        )

    def near_arrivals():
        a, b = lpan.at[y_dn, my_share], lpan.at[y_up, my_share]
        return (
            send(a, a, ly_s.at[0], ly_r.at[0], (z, y_up, d)),
            send(b, b, ly_s.at[1], ly_r.at[1], (z, y_dn, d)),
        )

    def far_copies():
        a, b = lpan.at[y_dn, first_part], lpan.at[y_up, second_part]
        return (
            send(a, a, ly_s.at[2], ly_r.at[2], (z, y_up, d)),
            send(b, b, ly_s.at[3], ly_r.at[3], (z, y_dn, d)),
        )

    def far_arrivals():
        a, b = lpan.at[y_far, first_part], lpan.at[y_far, second_part]
        return (
            send(a, a, ly_s.at[2], ly_r.at[2], (z, y_up, d)),
            send(b, b, ly_s.at[3], ly_r.at[3], (z, y_dn, d)),
        )

    def twin_copy(n, col, part):
        ref = lpan.at[col, part]
        return send(ref, ref, lc_s.at[n], lc_r.at[n], (z, y, twin))

    for c in near_copies():
        c.start()
    own_left = pltpu.make_async_copy(left, lpan.at[y], own_sem.at[0])
    own_right = pltpu.make_async_copy(right.at[:, my_cols], rpan.at[z], own_sem.at[1])
    own_left.start()
    own_right.start()
    out[...] = jnp.zeros_like(out)

    def add_product(chunk):
        col = chunk // per_col
        at = pl.ds(pl.multiple_of(lax.rem(chunk, per_col) * depth, 128), depth)
        out[...] += jnp.dot(
            lpan[col, :, at], rpan[chunk], preferred_element_type=jnp.float32
        )

    def entry_chunk(e):
        distance = (e + 1) // 2
        sign = 1 - 2 * lax.rem(e, 2)
        return lax.rem(z + sign * distance + rows, rows)

    per_step = -(-(rows - 1) // (half_steps - LEFT_READY))

    def ring_step(step, carry):
        for i in range(PIECES):
            up_arrival(step, i).wait_recv()
            if i < PIECES // 2:
                up_copy(step + 1, i).start()
            else:
                @pl.when(step < half_steps - 1)
                def _():
                    up_copy(step + 1, i).start()
            dn_arrival(step, i).wait_recv()
            if i < PIECES // 2:
                dn_copy(step + 1, i).start()
            else:
                @pl.when(step < half_steps - 1)
                def _():
                    dn_copy(step + 1, i).start()

        @pl.when(step == LEFT_NEAR)
        def _():
            for c in near_arrivals():
                c.wait_recv()
            for c in far_copies():
                c.start()
            twin_copy(0, y_dn, my_share).start()
            twin_copy(1, y_up, my_share).start()

        @pl.when(step == LEFT_FAR)
        def _():
            for c in far_arrivals():
                c.wait_recv()
            twin_copy(2, y_far, my_share).start()

        @pl.when(step == LEFT_READY)
        def _():
            own_left.wait()
            own_right.wait()
            for n, col in enumerate((y_dn, y_up, y_far)):
                twin_copy(n, col, twin_share).wait_recv()

        lo = jnp.maximum(step - LEFT_READY, 0) * per_step
        hi = jnp.minimum(jnp.maximum(step - LEFT_READY + 1, 0) * per_step, rows - 1)

        def body(e, c):
            add_product(entry_chunk(e))
            return c

        lax.fori_loop(lo, hi, body, 0)

        for i in range(PIECES):
            up_copy(step, i).wait_send()
            dn_copy(step, i).wait_send()
        return carry

    lax.fori_loop(1, half_steps, ring_step, 0)

    for c in near_copies() + far_copies():
        c.wait_send()
    for n, col in enumerate((y_dn, y_up, y_far)):
        twin_copy(n, col, my_share).wait_send()
    for i in range(PIECES // 2):
        up_arrival(half_steps, i).wait_recv()
        dn_arrival(half_steps, i).wait_recv()
    add_product(lax.rem(z + half_steps, rows))
    for i in range(PIECES // 2):
        up_copy(half_steps, i).wait_send()
        dn_copy(half_steps, i).wait_send()


def on_device(left_block, right_block):
    rows, cols = lax.axis_size("row"), lax.axis_size("col")
    layers = lax.axis_size("depth")
    height, left_cols = left_block.shape
    depth, right_cols = right_block.shape
    width = right_cols // layers
    steps = rows // 2 + 1
    dma = pltpu.SemaphoreType.DMA
    return pl.pallas_call(
        kernel,
        out_shape=jax.ShapeDtypeStruct((height, width), jnp.float32),
        in_specs=[pl.BlockSpec(memory_space=pl.ANY)] * 2,
        out_specs=pl.BlockSpec(memory_space=pltpu.VMEM),
        scratch_shapes=[
            pltpu.VMEM((cols, height, left_cols), jnp.bfloat16),
            pltpu.VMEM((rows, depth, width), jnp.bfloat16),
            dma((2,)),
            dma((steps, PIECES)),
            dma((steps, PIECES)),
            dma((steps, PIECES)),
            dma((steps, PIECES)),
            dma((4,)),
            dma((4,)),
            dma((3,)),
            dma((3,)),
        ],
        compiler_params=pltpu.CompilerParams(
            collective_id=0, has_side_effects=True, vmem_limit_bytes=48 << 20
        ),
        cost_estimate=pl.CostEstimate(
            flops=2 * height * width * depth * rows,
            bytes_accessed=2 * height * left_cols + 2 * depth * width + 4 * height * width,
            transcendentals=0,
        ),
    )(left_block, right_block)


def solution(mesh):
    return jax.shard_map(
        on_device,
        mesh=mesh,
        in_specs=(P("row", "col"), P("row", "col")),
        out_specs=P("row", ("col", "depth")),
        check_vma=False,
    )
```

```python
import functools

import jax
import jax.numpy as jnp
from jax import lax
from jax.experimental import pallas as pl
from jax.experimental.pallas import tpu as pltpu
from jax.sharding import PartitionSpec as P

PIECES = 4
LEFT_NEAR = 3
LEFT_FAR = 4
LEFT_READY = 5


def kernel(
    left, right, out, lpan, rpan,
    answer, own_sem, up_s, up_r, dn_s, dn_r, ly_s, ly_r, lc_s, lc_r,
):
    rows = lax.axis_size("row")
    cols = lax.axis_size("col")
    z, y, d = lax.axis_index("row"), lax.axis_index("col"), lax.axis_index("depth")
    depth, width = rpan.shape[1:]
    height = left.shape[0]
    half_steps = rows // 2
    piece = depth // PIECES
    per_col = left.shape[1] // depth

    z_up, z_dn = lax.rem(z + 1, rows), lax.rem(z + rows - 1, rows)
    y_up, y_dn = lax.rem(y + 1, cols), lax.rem(y + cols - 1, cols)
    y_far = lax.rem(y + 2, cols)
    core = lax.rem(d, 2)
    twin = d + 1 - 2 * core

    my_cols = pl.ds(pl.multiple_of(d * width, 128), width)
    own_right = pltpu.make_async_copy(right.at[:, my_cols], rpan.at[z], own_sem.at[1])
    own_left = pltpu.make_async_copy(left, lpan.at[y], own_sem.at[0])
    own_right.start()
    own_left.start()

    turned = jnp.logical_and(z == 0, d == 0)
    up, dn, right_of, left_of, beside = range(5)
    peers = ((z_up, y, d), (z_dn, y, d), (z, y_up, d), (z, y_dn, d), (z, y, twin))
    greets = (
        z != rows - 1,
        z == 0,
        jnp.logical_xor(y != cols - 1, turned),
        jnp.logical_xor(y == 0, turned),
        core == 1,
    )
    back = (dn, up, left_of, right_of, beside)

    barrier = pltpu.get_barrier_semaphore()
    greeted = 0
    for who, first in zip(peers, greets):
        greeted = greeted + jnp.where(first, 0, 1)

        @pl.when(first)
        def _():
            pl.semaphore_signal(barrier, inc=1, device_id=who)

    @pl.when(greeted > 0)
    def _():
        pl.semaphore_wait(barrier, greeted)

    for side, (who, first) in enumerate(zip(peers, greets)):
        @pl.when(jnp.logical_not(first))
        def _():
            pl.semaphore_signal(answer.at[back[side]], inc=1, device_id=who)

    def admitted(side):
        @pl.when(greets[side])
        def _():
            pl.semaphore_wait(answer.at[side], 1)

    def up_rows(i):
        return pl.ds(i * piece, piece)

    def dn_rows(i):
        return pl.ds((i + PIECES // 2) % PIECES * piece, piece)

    def send(src, dst, send_sem, recv_sem, who):
        return pltpu.make_async_remote_copy(
            src_ref=src, dst_ref=dst, send_sem=send_sem, recv_sem=recv_sem,
            device_id=who,
        )

    def up_copy(step, i):
        chunk = lax.rem(z - step + 1 + rows, rows)
        dst = rpan.at[chunk, up_rows(i)]
        return send(dst, dst, up_s.at[step, i], up_r.at[step, i], (z_up, y, d))

    def dn_copy(step, i):
        chunk = lax.rem(z + step - 1, rows)
        dst = rpan.at[chunk, dn_rows(i)]
        return send(dst, dst, dn_s.at[step, i], dn_r.at[step, i], (z_dn, y, d))

    def up_arrival(step, i):
        dst = rpan.at[lax.rem(z - step + rows, rows), up_rows(i)]
        return send(dst, dst, up_s.at[step, i], up_r.at[step, i], (z_up, y, d))

    def dn_arrival(step, i):
        dst = rpan.at[lax.rem(z + step, rows), dn_rows(i)]
        return send(dst, dst, dn_s.at[step, i], dn_r.at[step, i], (z_dn, y, d))

    def start_dn():
        admitted(dn)
        for i in range(PIECES):
            dn_copy(1, i).start()

    own_right.wait()

    @pl.when(z != 0)
    def _():
        start_dn()

    admitted(up)
    for i in range(PIECES):
        up_copy(1, i).start()

    share = height // 2
    my_share = pl.ds(pl.multiple_of(core * share, 16), share)
    twin_share = pl.ds(pl.multiple_of((1 - core) * share, 16), share)
    first_part = pl.ds(pl.multiple_of(core * share, 16), share // 2)
    second_part = pl.ds(pl.multiple_of(core * share + share // 2, 16), share // 2)

    def near_copies():
        src = dst = lpan.at[y, my_share]
        return (
            send(src, dst, ly_s.at[0], ly_r.at[0], (z, y_up, d)),
            send(src, dst, ly_s.at[1], ly_r.at[1], (z, y_dn, d)),
        )

    def near_arrivals():
        a, b = lpan.at[y_dn, my_share], lpan.at[y_up, my_share]
        return (
            send(a, a, ly_s.at[0], ly_r.at[0], (z, y_up, d)),
            send(b, b, ly_s.at[1], ly_r.at[1], (z, y_dn, d)),
        )

    def far_copies():
        a, b = lpan.at[y_dn, first_part], lpan.at[y_up, second_part]
        return (
            send(a, a, ly_s.at[2], ly_r.at[2], (z, y_up, d)),
            send(b, b, ly_s.at[3], ly_r.at[3], (z, y_dn, d)),
        )

    def far_arrivals():
        a, b = lpan.at[y_far, first_part], lpan.at[y_far, second_part]
        return (
            send(a, a, ly_s.at[2], ly_r.at[2], (z, y_up, d)),
            send(b, b, ly_s.at[3], ly_r.at[3], (z, y_dn, d)),
        )

    def twin_copy(n, col, part):
        ref = lpan.at[col, part]
        return send(ref, ref, lc_s.at[n], lc_r.at[n], (z, y, twin))

    own_left.wait()
    admitted(right_of)
    admitted(left_of)
    for c in near_copies():
        c.start()
    out[...] = jnp.zeros_like(out)

    @pl.when(z == 0)
    def _():
        start_dn()

    def add_product(chunk):
        col = chunk // per_col
        at = pl.ds(pl.multiple_of(lax.rem(chunk, per_col) * depth, 128), depth)
        out[...] += jnp.dot(
            lpan[col, :, at], rpan[chunk], preferred_element_type=jnp.float32
        )

    def entry_chunk(e):
        distance = (e + 1) // 2
        sign = 1 - 2 * lax.rem(e, 2)
        return lax.rem(z + sign * distance + rows, rows)

    per_step = -(-(rows - 1) // (half_steps - LEFT_READY))

    def last_up(at, i):
        return at != 0 if i < PIECES // 2 else False

    def last_dn(at, i):
        return True if i < PIECES // 2 else at == 0

    def ring_step(step, carry):
        for i in range(PIECES):
            up_arrival(step, i).wait_recv()

            @pl.when(jnp.logical_or(step < half_steps - 1, last_up(z_up, i)))
            def _():
                up_copy(step + 1, i).start()

            dn_arrival(step, i).wait_recv()

            @pl.when(jnp.logical_or(step < half_steps - 1, last_dn(z_dn, i)))
            def _():
                dn_copy(step + 1, i).start()


        @pl.when(step == LEFT_NEAR)
        def _():
            for c in near_arrivals():
                c.wait_recv()
            for c in far_copies():
                c.start()
            admitted(beside)
            twin_copy(0, y_dn, my_share).start()
            twin_copy(1, y_up, my_share).start()

        @pl.when(step == LEFT_FAR)
        def _():
            for c in far_arrivals():
                c.wait_recv()
            twin_copy(2, y_far, my_share).start()

        @pl.when(step == LEFT_READY)
        def _():
            for n, col in enumerate((y_dn, y_up, y_far)):
                twin_copy(n, col, twin_share).wait_recv()

        lo = jnp.maximum(step - LEFT_READY, 0) * per_step
        hi = jnp.minimum(jnp.maximum(step - LEFT_READY + 1, 0) * per_step, rows - 1)

        def body(e, c):
            add_product(entry_chunk(e))
            return c

        lax.fori_loop(lo, hi, body, 0)

        for i in range(PIECES):
            up_copy(step, i).wait_send()
            dn_copy(step, i).wait_send()
        return carry

    lax.fori_loop(1, half_steps, ring_step, 0)

    for c in near_copies() + far_copies():
        c.wait_send()
    for n, col in enumerate((y_dn, y_up, y_far)):
        twin_copy(n, col, my_share).wait_send()
    for i in range(PIECES):
        @pl.when(last_up(z, i))
        def _():
            up_arrival(half_steps, i).wait_recv()

        @pl.when(last_dn(z, i))
        def _():
            dn_arrival(half_steps, i).wait_recv()

    add_product(lax.rem(z + half_steps, rows))
    for i in range(PIECES):
        @pl.when(last_up(z_up, i))
        def _():
            up_copy(half_steps, i).wait_send()

        @pl.when(last_dn(z_dn, i))
        def _():
            dn_copy(half_steps, i).wait_send()


def on_device(left_block, right_block):
    rows, cols = lax.axis_size("row"), lax.axis_size("col")
    layers = lax.axis_size("depth")
    height, left_cols = left_block.shape
    depth, right_cols = right_block.shape
    width = right_cols // layers
    steps = rows // 2 + 1
    dma = pltpu.SemaphoreType.DMA
    return pl.pallas_call(
        kernel,
        out_shape=pltpu.VMEM((height, width), jnp.float32),
        in_specs=[pl.BlockSpec(memory_space=pl.ANY)] * 2,
        out_specs=pl.BlockSpec(memory_space=pltpu.VMEM),
        scratch_shapes=[
            pltpu.VMEM((cols, height, left_cols), jnp.bfloat16),
            pltpu.VMEM((rows, depth, width), jnp.bfloat16),
            pltpu.SemaphoreType.REGULAR((5,)),
            dma((2,)),
            dma((steps, PIECES)),
            dma((steps, PIECES)),
            dma((steps, PIECES)),
            dma((steps, PIECES)),
            dma((4,)),
            dma((4,)),
            dma((3,)),
            dma((3,)),
        ],
        compiler_params=pltpu.CompilerParams(
            collective_id=0, has_side_effects=True, vmem_limit_bytes=63 << 20
        ),
        cost_estimate=pl.CostEstimate(
            flops=2 * height * width * depth * rows,
            bytes_accessed=2 * height * left_cols + 2 * depth * width + 4 * height * width,
            transcendentals=0,
        ),
    )(left_block, right_block)


def solution(mesh):
    return jax.shard_map(
        on_device,
        mesh=mesh,
        in_specs=(P("row", "col"), P("row", "col")),
        out_specs=P("row", ("col", "depth")),
        check_vma=False,
    )
```

```python
import functools

import jax
import jax.numpy as jnp
from jax import lax
from jax.experimental import pallas as pl
from jax.experimental.pallas import tpu as pltpu
from jax.sharding import PartitionSpec as P

PIECES = 4
FROM_BELOW = {0: 28, 1: 29, 15: 32}
LAG = {0: 4, 1: 2, 2: 1}
LEFT_NEAR = 3
LEFT_FAR = 4
LEFT_READY = 5


def kernel(
    left, right, out, lpan, rpan,
    answer, own_sem, up_s, up_r, dn_s, dn_r, ly_s, ly_r, lc_s, lc_r,
):
    rows = lax.axis_size("row")
    cols = lax.axis_size("col")
    z, y, d = lax.axis_index("row"), lax.axis_index("col"), lax.axis_index("depth")
    depth, width = rpan.shape[1:]
    height = left.shape[0]
    half_steps = rows // 2
    piece = depth // PIECES
    per_col = left.shape[1] // depth

    z_up, z_dn = lax.rem(z + 1, rows), lax.rem(z + rows - 1, rows)
    y_up, y_dn = lax.rem(y + 1, cols), lax.rem(y + cols - 1, cols)
    y_far = lax.rem(y + 2, cols)
    core = lax.rem(d, 2)
    twin = d + 1 - 2 * core

    my_cols = pl.ds(pl.multiple_of(d * width, 128), width)
    own_right = pltpu.make_async_copy(right.at[:, my_cols], rpan.at[z], own_sem.at[1])
    own_left = pltpu.make_async_copy(left, lpan.at[y], own_sem.at[0])
    own_right.start()
    own_left.start()

    turned = jnp.logical_and(z == 0, d == 0)
    up, dn, right_of, left_of, beside = range(5)
    peers = ((z_up, y, d), (z_dn, y, d), (z, y_up, d), (z, y_dn, d), (z, y, twin))
    greets = (
        z != rows - 1,
        z == 0,
        jnp.logical_xor(y != cols - 1, turned),
        jnp.logical_xor(y == 0, turned),
        core == 1,
    )
    back = (dn, up, left_of, right_of, beside)

    barrier = pltpu.get_barrier_semaphore()
    greeted = 0
    for who, first in zip(peers, greets):
        greeted = greeted + jnp.where(first, 0, 1)

        @pl.when(first)
        def _():
            pl.semaphore_signal(barrier, inc=1, device_id=who)

    @pl.when(greeted > 0)
    def _():
        pl.semaphore_wait(barrier, greeted)

    for side, (who, first) in enumerate(zip(peers, greets)):
        @pl.when(jnp.logical_not(first))
        def _():
            pl.semaphore_signal(answer.at[back[side]], inc=1, device_id=who)

    def admitted(side):
        @pl.when(greets[side])
        def _():
            pl.semaphore_wait(answer.at[side], 1)

    def part(i):
        return pl.ds(pl.multiple_of(i * piece, 16), piece)

    def send(src, dst, send_sem, recv_sem, who):
        return pltpu.make_async_remote_copy(
            src_ref=src, dst_ref=dst, send_sem=send_sem, recv_sem=recv_sem,
            device_id=who,
        )

    def up_copy(at):
        chunk = lax.rem(z - at // PIECES + rows, rows)
        ref = rpan.at[chunk, part(lax.rem(at, PIECES))]
        return send(ref, ref, up_s.at[at], up_r.at[at], (z_up, y, d))

    def dn_copy(at):
        chunk = lax.rem(z + at // PIECES, rows)
        ref = rpan.at[chunk, part(PIECES - 1 - lax.rem(at, PIECES))]
        return send(ref, ref, dn_s.at[at], dn_r.at[at], (z_dn, y, d))

    def up_arrival(at):
        chunk = lax.rem(z - at // PIECES - 1 + rows, rows)
        ref = rpan.at[chunk, part(lax.rem(at, PIECES))]
        return send(ref, ref, up_s.at[at], up_r.at[at], (z_up, y, d))

    def dn_arrival(at):
        chunk = lax.rem(z + at // PIECES + 1, rows)
        ref = rpan.at[chunk, part(PIECES - 1 - lax.rem(at, PIECES))]
        return send(ref, ref, dn_s.at[at], dn_r.at[at], (z_dn, y, d))

    def start_dn():
        admitted(dn)
        for i in range(PIECES):
            dn_copy(i).start()

    own_right.wait()

    @pl.when(z != 0)
    def _():
        start_dn()

    admitted(up)
    for i in range(PIECES):
        up_copy(i).start()

    share = height // 2
    my_share = pl.ds(pl.multiple_of(core * share, 16), share)
    twin_share = pl.ds(pl.multiple_of((1 - core) * share, 16), share)
    first_part = pl.ds(pl.multiple_of(core * share, 16), share // 2)
    second_part = pl.ds(pl.multiple_of(core * share + share // 2, 16), share // 2)

    def near_copies():
        src = dst = lpan.at[y, my_share]
        return (
            send(src, dst, ly_s.at[0], ly_r.at[0], (z, y_up, d)),
            send(src, dst, ly_s.at[1], ly_r.at[1], (z, y_dn, d)),
        )

    def near_arrivals():
        a, b = lpan.at[y_dn, my_share], lpan.at[y_up, my_share]
        return (
            send(a, a, ly_s.at[0], ly_r.at[0], (z, y_up, d)),
            send(b, b, ly_s.at[1], ly_r.at[1], (z, y_dn, d)),
        )

    def far_copies():
        a, b = lpan.at[y_dn, first_part], lpan.at[y_up, second_part]
        return (
            send(a, a, ly_s.at[2], ly_r.at[2], (z, y_up, d)),
            send(b, b, ly_s.at[3], ly_r.at[3], (z, y_dn, d)),
        )

    def far_arrivals():
        a, b = lpan.at[y_far, first_part], lpan.at[y_far, second_part]
        return (
            send(a, a, ly_s.at[2], ly_r.at[2], (z, y_up, d)),
            send(b, b, ly_s.at[3], ly_r.at[3], (z, y_dn, d)),
        )

    def twin_copy(n, col, part):
        ref = lpan.at[col, part]
        return send(ref, ref, lc_s.at[n], lc_r.at[n], (z, y, twin))

    own_left.wait()
    admitted(right_of)
    admitted(left_of)
    for c in near_copies():
        c.start()
    out[...] = jnp.zeros_like(out)

    @pl.when(z == 0)
    def _():
        start_dn()

    def add_product(chunk):
        col = chunk // per_col
        at = pl.ds(pl.multiple_of(lax.rem(chunk, per_col) * depth, 128), depth)
        out[...] += jnp.dot(
            lpan[col, :, at], rpan[chunk], preferred_element_type=jnp.float32
        )

    def entry_chunk(e):
        distance = (e + 1) // 2
        sign = 2 * lax.rem(e, 2) - 1
        return lax.rem(z + sign * distance + rows, rows)

    total = (rows - 1) * PIECES

    def below(at):
        count = total // 2
        for plane, pieces in FROM_BELOW.items():
            count = jnp.where(at == plane, pieces, count)
        return count

    mine_up, mine_dn = below(z), total - below(z)
    next_up, next_dn = below(z_up), total - below(z_dn)
    lag = 0
    for plane, pieces in LAG.items():
        lag = jnp.where(z == plane, pieces, lag)

    def ring_step(step):
        for i in range(PIECES):
            at_dn = (step - 1) * PIECES + i
            at_up = at_dn - lag

            @pl.when(jnp.logical_and(at_up >= 0, at_up < mine_up))
            def _():
                up_arrival(at_up).wait_recv()

                @pl.when(at_up + PIECES < next_up)
                def _():
                    up_copy(at_up + PIECES).start()

            @pl.when(at_dn < mine_dn)
            def _():
                dn_arrival(at_dn).wait_recv()

                @pl.when(at_dn + PIECES < next_dn)
                def _():
                    dn_copy(at_dn + PIECES).start()

    def sent(step):
        for i in range(PIECES):
            at = (step - 1) * PIECES + i

            @pl.when(at < next_up)
            def _():
                up_copy(at).wait_send()

            @pl.when(at < next_dn)
            def _():
                dn_copy(at).wait_send()

    near = half_steps - 2
    entries = 2 * near
    per_step = -(-entries // (near - LEFT_READY + 1))

    def near_step(step, carry):
        ring_step(step)

        @pl.when(step == LEFT_NEAR)
        def _():
            for c in near_arrivals():
                c.wait_recv()
            for c in far_copies():
                c.start()
            admitted(beside)
            twin_copy(0, y_dn, my_share).start()
            twin_copy(1, y_up, my_share).start()

        @pl.when(step == LEFT_FAR)
        def _():
            for c in far_arrivals():
                c.wait_recv()
            twin_copy(2, y_far, my_share).start()

        @pl.when(step == LEFT_READY)
        def _():
            for n, col in enumerate((y_dn, y_up, y_far)):
                twin_copy(n, col, twin_share).wait_recv()

        lo = jnp.maximum(step - LEFT_READY, 0) * per_step
        hi = jnp.minimum(jnp.maximum(step - LEFT_READY + 1, 0) * per_step, entries)

        def body(e, c):
            add_product(entry_chunk(e))
            return c

        lax.fori_loop(lo, hi, body, 0)

        @pl.when(step > 1)
        def _():
            sent(step - 1)

        return carry

    lax.fori_loop(1, near + 1, near_step, 0)

    def far_step(step, carry):
        ring_step(step)
        sent(step - 1)

        @pl.when(step == near + 1)
        def _():
            for c in near_copies() + far_copies():
                c.wait_send()
            for n, col in enumerate((y_dn, y_up, y_far)):
                twin_copy(n, col, my_share).wait_send()

        def body(e, c):
            add_product(entry_chunk(e))
            return c

        count = jnp.where(lag == 0, 3, 2)
        lo = jnp.where(step == near + 1, 0, jnp.where(step == near + 3, count, 3))
        hi = jnp.where(step == near + 1, count, jnp.where(step == near + 3, 4, 3))
        lax.fori_loop(entries + lo, entries + hi, body, 0)
        return carry

    lax.fori_loop(near + 1, near + 4, far_step, 0)
    sent(near + 3)


def on_device(left_block, right_block):
    rows, cols = lax.axis_size("row"), lax.axis_size("col")
    layers = lax.axis_size("depth")
    height, left_cols = left_block.shape
    depth, right_cols = right_block.shape
    width = right_cols // layers
    order = (rows // 2 + 1) * PIECES
    dma = pltpu.SemaphoreType.DMA
    return pl.pallas_call(
        kernel,
        out_shape=pltpu.VMEM((height, width), jnp.float32),
        in_specs=[pl.BlockSpec(memory_space=pl.ANY)] * 2,
        out_specs=pl.BlockSpec(memory_space=pltpu.VMEM),
        scratch_shapes=[
            pltpu.VMEM((cols, height, left_cols), jnp.bfloat16),
            pltpu.VMEM((rows, depth, width), jnp.bfloat16),
            pltpu.SemaphoreType.REGULAR((5,)),
            dma((2,)),
            dma((order,)),
            dma((order,)),
            dma((order,)),
            dma((order,)),
            dma((4,)),
            dma((4,)),
            dma((3,)),
            dma((3,)),
        ],
        compiler_params=pltpu.CompilerParams(
            collective_id=0, has_side_effects=True, vmem_limit_bytes=63 << 20
        ),
        cost_estimate=pl.CostEstimate(
            flops=2 * height * width * depth * rows,
            bytes_accessed=2 * height * left_cols + 2 * depth * width + 4 * height * width,
            transcendentals=0,
        ),
    )(left_block, right_block)


def solution(mesh):
    return jax.shard_map(
        on_device,
        mesh=mesh,
        in_specs=(P("row", "col"), P("row", "col")),
        out_specs=P("row", ("col", "depth")),
        check_vma=False,
    )
```

```python
import functools

import jax
import jax.numpy as jnp
from jax import lax
from jax.experimental import pallas as pl
from jax.experimental.pallas import tpu as pltpu
from jax.sharding import PartitionSpec as P

PIECES = 4
TAKES = 3 * PIECES + 1
FROM_BELOW = {0: (27, 28), 1: (28, 28), 15: (32, 32)}
LAG = {0: 4, 1: 3, 2: 2, 3: 1}
LEFT_NEAR = 3
LEFT_FAR = 4
LEFT_READY = 5
PER_TURN = 2


def kernel(
    left, right, out, lpan, rpan,
    answer, own_sem, up_s, up_r, dn_s, dn_r, left_s, left_r,
):
    rows = lax.axis_size("row")
    cols = lax.axis_size("col")
    z, y, d = lax.axis_index("row"), lax.axis_index("col"), lax.axis_index("depth")
    depth, width = right.shape[0], rpan.shape[1]
    height = left.shape[0]
    half_steps = rows // 2
    piece = depth // PIECES
    per_col = left.shape[1] // depth

    z_up, z_dn = lax.rem(z + 1, rows), lax.rem(z + rows - 1, rows)
    y_up, y_dn = lax.rem(y + 1, cols), lax.rem(y + cols - 1, cols)
    y_far = lax.rem(y + 2, cols)
    core = lax.rem(d, 2)
    twin = d + 1 - 2 * core

    def chunk_rows(chunk, first=0, size=depth):
        return rpan.at[pl.ds(pl.multiple_of(chunk * depth + first, 16), size)]

    def left_rows(col, first=0, size=height):
        return lpan.at[pl.ds(pl.multiple_of(col * height + first, 16), size)]

    my_cols = pl.ds(pl.multiple_of(d * width, 128), width)
    own_right = pltpu.make_async_copy(right.at[:, my_cols], chunk_rows(z), own_sem.at[1])
    own_left = pltpu.make_async_copy(left, left_rows(y), own_sem.at[0])
    own_right.start()
    own_left.start()

    turned = jnp.logical_and(z == 0, d == 0)
    up, dn, right_of, left_of, beside = range(5)
    peers = ((z_up, y, d), (z_dn, y, d), (z, y_up, d), (z, y_dn, d), (z, y, twin))
    greets = (
        z < rows - 2,
        jnp.logical_or(z == 0, z == rows - 1),
        jnp.logical_xor(y != cols - 1, turned),
        jnp.logical_xor(y == 0, turned),
        core == 1,
    )
    back = (dn, up, left_of, right_of, beside)

    barrier = pltpu.get_barrier_semaphore()
    greeted = 0
    for who, first in zip(peers, greets):
        greeted = greeted + jnp.where(first, 0, 1)

        @pl.when(first)
        def _():
            pl.semaphore_signal(barrier, inc=1, device_id=who)

    @pl.when(greeted > 0)
    def _():
        pl.semaphore_wait(barrier, greeted)

    for side, (who, first) in enumerate(zip(peers, greets)):
        @pl.when(jnp.logical_not(first))
        def _():
            pl.semaphore_signal(answer.at[back[side]], inc=1, device_id=who)

    def admitted(side):
        @pl.when(greets[side])
        def _():
            pl.semaphore_wait(answer.at[side], 1)

    def part(chunk, i):
        return chunk_rows(chunk, i * piece, piece)

    def send(src, dst, send_sem, recv_sem, who):
        return pltpu.make_async_remote_copy(
            src_ref=src, dst_ref=dst, send_sem=send_sem, recv_sem=recv_sem,
            device_id=who,
        )

    def up_copy(at):
        chunk = lax.rem(z - at // PIECES + rows, rows)
        ref = part(chunk, lax.rem(at, PIECES))
        src = right.at[pl.ds(at * piece, piece), my_cols] if isinstance(at, int) else ref
        return send(src, ref, up_s.at[0], up_r.at[at % TAKES], (z_up, y, d))

    def dn_copy(at):
        chunk = lax.rem(z + at // PIECES, rows)
        ref = part(chunk, PIECES - 1 - lax.rem(at, PIECES))
        src = right.at[pl.ds((PIECES - 1 - at) * piece, piece), my_cols] if isinstance(at, int) else ref
        return send(src, ref, dn_s.at[0], dn_r.at[at % TAKES], (z_dn, y, d))

    def up_arrival(at):
        chunk = lax.rem(z - at // PIECES - 1 + rows, rows)
        ref = part(chunk, lax.rem(at, PIECES))
        return send(ref, ref, up_s.at[0], up_r.at[at % TAKES], (z_up, y, d))

    def dn_arrival(at):
        chunk = lax.rem(z + at // PIECES + 1, rows)
        ref = part(chunk, PIECES - 1 - lax.rem(at, PIECES))
        return send(ref, ref, dn_s.at[0], dn_r.at[at % TAKES], (z_dn, y, d))

    def start_dn():
        admitted(dn)
        for i in range(PIECES):
            dn_copy(i).start()

    outer = jnp.logical_or(z == 0, z == rows - 1)

    @pl.when(jnp.logical_not(outer))
    def _():
        start_dn()

    admitted(up)
    for i in range(PIECES):
        up_copy(i).start()

    @pl.when(z == rows - 1)
    def _():
        start_dn()

    share = height // 2
    mine = core * share
    to_right, to_left, to_twin = (z, y_up, d), (z, y_dn, d), (z, y, twin)

    def near_copies():
        ref = left_rows(y, mine, share)
        return (
            send(ref, ref, left_s.at[0], left_r.at[0], to_right),
            send(ref, ref, left_s.at[0], left_r.at[0], to_left),
        )

    def far_copies():
        a = left_rows(y_dn, mine, share // 2)
        b = left_rows(y_up, mine + share // 2, share // 2)
        return (
            send(a, a, left_s.at[0], left_r.at[1], to_right),
            send(b, b, left_s.at[0], left_r.at[1], to_left),
        )

    def twin_copy(col):
        ref = left_rows(col, mine, share)
        return send(ref, ref, left_s.at[1], left_r.at[2], to_twin)

    def all_of(size, which_s, which_r):
        ref = lpan.at[pl.ds(0, size)]
        return send(ref, ref, left_s.at[which_s], left_r.at[which_r], to_twin)

    own_left.wait()
    own_right.wait()
    admitted(right_of)
    admitted(left_of)
    for c in near_copies():
        c.start()
    out[...] = jnp.zeros_like(out)

    @pl.when(z == 0)
    def _():
        start_dn()

    def add_product(chunk):
        col = chunk // per_col
        at = pl.ds(pl.multiple_of(lax.rem(chunk, per_col) * depth, 128), depth)
        out[...] += jnp.dot(
            left_rows(col)[:, at], chunk_rows(chunk)[...], preferred_element_type=jnp.float32
        )

    total = (rows - 1) * PIECES

    def below(at):
        count = total // 2
        for plane, pieces in FROM_BELOW.items():
            count = jnp.where(at == plane, jnp.where(core == 0, *pieces), count)
        return count

    mine_up, mine_dn = below(z), total - below(z)
    next_up, next_dn = below(z_up), total - below(z_dn)
    lag = 0
    for plane, pieces in LAG.items():
        lag = jnp.where(z == plane, pieces, lag)

    def all_sent(count, sem, counts):
        for n in sorted(counts):
            ref = rpan.at[pl.ds(0, n * piece)]

            @pl.when(count == n)
            def _():
                send(ref, ref, sem.at[0], up_r.at[0], (z_up, y, d)).wait_send()

    seven = half_steps - 1
    whole_7 = jnp.where(mine_up >= seven * PIECES, seven * PIECES - 1 + lag, mine_dn - 1)
    whole_8 = jnp.where(
        mine_dn >= half_steps * PIECES,
        half_steps * PIECES - 1,
        jnp.maximum(mine_up - 1 + lag, mine_dn - 1),
    )
    turn_round = whole_8 < whole_7
    whole_first = jnp.minimum(whole_7, whole_8)
    whole_second = jnp.maximum(whole_7, whole_8)
    regular = 2 * seven

    def entry_chunk(e):
        e = jnp.where(jnp.logical_and(turn_round, e >= regular), 2 * regular + 1 - e, e)
        distance = (e + 1) // 2
        sign = 2 * lax.rem(e, 2) - 1
        return lax.rem(z + sign * distance + rows, rows)

    def whole_after(at):
        from_above = jnp.minimum((at + 1) // PIECES, seven)
        from_below = jnp.clip((at + 1 - lag) // PIECES, 0, seven - 1)
        count = 2 * from_below + jnp.where(from_above > from_below, 2, 1)
        more = jnp.where(at >= whole_first, 1, 0) + jnp.where(at >= whole_second, 1, 0)
        return count + jnp.where(count == regular, more, 0)

    turns = jnp.maximum(mine_up + lag, mine_dn)

    def take(at, done):
        at_up = at - lag

        @pl.when(jnp.logical_and(at_up >= 0, at_up < mine_up))
        def _():
            up_arrival(at_up).wait_recv()

            @pl.when(at_up + PIECES < next_up)
            def _():
                up_copy(at_up + PIECES).start()

        @pl.when(at < mine_dn)
        def _():
            dn_arrival(at).wait_recv()

            @pl.when(at + PIECES < next_dn)
            def _():
                dn_copy(at + PIECES).start()

        @pl.when(at == LEFT_NEAR * PIECES)
        def _():
            all_of(2 * share, 0, 0).wait_recv()
            for c in far_copies():
                c.start()
            admitted(beside)
            twin_copy(y_dn).start()
            twin_copy(y_up).start()

        @pl.when(at == LEFT_FAR * PIECES)
        def _():
            all_of(share, 0, 1).wait_recv()
            twin_copy(y_far).start()

        @pl.when(at == LEFT_READY * PIECES)
        def _():
            all_of(3 * share, 1, 2).wait_recv()
            all_of(3 * share, 0, 0).wait_send()
            all_of(3 * share, 1, 0).wait_send()

        whole = jnp.where(at < LEFT_READY * PIECES, 0, whole_after(at))
        upto = jnp.where(at == turns - 1, whole, jnp.minimum(whole, done + PER_TURN))

        def body(e, c):
            add_product(entry_chunk(e))
            return c

        lax.fori_loop(done, upto, body, 0)
        return upto

    lax.fori_loop(0, turns, take, 0)
    counts = {total // 2}.union(*FROM_BELOW.values())
    all_sent(next_up, up_s, counts)
    all_sent(next_dn, dn_s, {total - n for n in counts})


def on_device(left_block, right_block):
    rows, cols = lax.axis_size("row"), lax.axis_size("col")
    layers = lax.axis_size("depth")
    height, left_cols = left_block.shape
    depth, right_cols = right_block.shape
    width = right_cols // layers
    dma = pltpu.SemaphoreType.DMA
    return pl.pallas_call(
        kernel,
        out_shape=pltpu.VMEM((height, width), jnp.float32),
        in_specs=[pl.BlockSpec(memory_space=pl.ANY)] * 2,
        out_specs=pl.BlockSpec(memory_space=pltpu.VMEM),
        scratch_shapes=[
            pltpu.VMEM((cols * height, left_cols), jnp.bfloat16),
            pltpu.VMEM((rows * depth, width), jnp.bfloat16),
            pltpu.SemaphoreType.REGULAR((5,)),
            dma((2,)),
            dma((1,)),
            dma((TAKES,)),
            dma((1,)),
            dma((TAKES,)),
            dma((2,)),
            dma((3,)),
        ],
        compiler_params=pltpu.CompilerParams(
            collective_id=0, has_side_effects=True, vmem_limit_bytes=63 << 20
        ),
        cost_estimate=pl.CostEstimate(
            flops=2 * height * width * depth * rows,
            bytes_accessed=2 * height * left_cols + 2 * depth * width + 4 * height * width,
            transcendentals=0,
        ),
    )(left_block, right_block)


def solution(mesh):
    return jax.shard_map(
        on_device,
        mesh=mesh,
        in_specs=(P("row", "col"), P("row", "col")),
        out_specs=P("row", ("col", "depth")),
        check_vma=False,
    )
```

```python
import functools

import jax
import jax.numpy as jnp
from jax import lax
from jax.experimental import pallas as pl
from jax.experimental.pallas import tpu as pltpu
from jax.sharding import PartitionSpec as P

PIECES = 4
TAKES = 3 * PIECES + 1
FROM_BELOW = {0: (27, 28), 1: (28, 28), 15: (32, 32)}
LAG = {0: 4, 1: 3, 2: 2, 3: 1}
LEFT_NEAR = 3
LEFT_FAR = 4
LEFT_READY = 5
PER_TURN = 2
BLOCK = 128


def kernel(
    left, right, out, lpan, rpan,
    answer, own_sem, up_s, up_r, dn_s, dn_r, left_s, left_r,
):
    rows = lax.axis_size("row")
    cols = lax.axis_size("col")
    z, y, d = lax.axis_index("row"), lax.axis_index("col"), lax.axis_index("depth")
    depth, width = right.shape[0], rpan.shape[1]
    height = left.shape[0]
    half_steps = rows // 2
    piece = depth // PIECES
    per_col = left.shape[1] // depth

    z_up, z_dn = lax.rem(z + 1, rows), lax.rem(z + rows - 1, rows)
    y_up, y_dn = lax.rem(y + 1, cols), lax.rem(y + cols - 1, cols)
    y_far = lax.rem(y + 2, cols)
    core = lax.rem(d, 2)
    twin = d + 1 - 2 * core

    def chunk_rows(chunk, first=0, size=depth):
        return rpan.at[pl.ds(pl.multiple_of(chunk * depth + first, 16), size)]

    def left_rows(col, first=0, size=height):
        return lpan.at[pl.ds(pl.multiple_of(col * height + first, 16), size)]

    my_cols = pl.ds(pl.multiple_of(d * width, 128), width)
    own_right = pltpu.make_async_copy(right.at[:, my_cols], chunk_rows(z), own_sem.at[1])
    own_left = pltpu.make_async_copy(left, left_rows(y), own_sem.at[0])
    own_right.start()
    own_left.start()

    turned = jnp.logical_and(z == 0, d == 0)
    up, dn, right_of, left_of, beside = range(5)
    peers = ((z_up, y, d), (z_dn, y, d), (z, y_up, d), (z, y_dn, d), (z, y, twin))
    greets = (
        z < rows - 2,
        jnp.logical_or(z == 0, z == rows - 1),
        jnp.logical_xor(y != cols - 1, turned),
        jnp.logical_xor(y == 0, turned),
        core == 1,
    )
    back = (dn, up, left_of, right_of, beside)

    barrier = pltpu.get_barrier_semaphore()
    greeted = 0
    for who, first in zip(peers, greets):
        greeted = greeted + jnp.where(first, 0, 1)

        @pl.when(first)
        def _():
            pl.semaphore_signal(barrier, inc=1, device_id=who)

    @pl.when(greeted > 0)
    def _():
        pl.semaphore_wait(barrier, greeted)

    for side, (who, first) in enumerate(zip(peers, greets)):
        @pl.when(jnp.logical_not(first))
        def _():
            pl.semaphore_signal(answer.at[back[side]], inc=1, device_id=who)

    def admitted(side):
        @pl.when(greets[side])
        def _():
            pl.semaphore_wait(answer.at[side], 1)

    def part(chunk, i):
        return chunk_rows(chunk, i * piece, piece)

    def send(src, dst, send_sem, recv_sem, who):
        return pltpu.make_async_remote_copy(
            src_ref=src, dst_ref=dst, send_sem=send_sem, recv_sem=recv_sem,
            device_id=who,
        )

    def up_copy(at):
        chunk = lax.rem(z - at // PIECES + rows, rows)
        ref = part(chunk, lax.rem(at, PIECES))
        src = right.at[pl.ds(at * piece, piece), my_cols] if isinstance(at, int) else ref
        return send(src, ref, up_s.at[0], up_r.at[at % TAKES], (z_up, y, d))

    def dn_copy(at):
        chunk = lax.rem(z + at // PIECES, rows)
        ref = part(chunk, PIECES - 1 - lax.rem(at, PIECES))
        src = right.at[pl.ds((PIECES - 1 - at) * piece, piece), my_cols] if isinstance(at, int) else ref
        return send(src, ref, dn_s.at[0], dn_r.at[at % TAKES], (z_dn, y, d))

    def up_arrival(at):
        chunk = lax.rem(z - at // PIECES - 1 + rows, rows)
        ref = part(chunk, lax.rem(at, PIECES))
        return send(ref, ref, up_s.at[0], up_r.at[at % TAKES], (z_up, y, d))

    def dn_arrival(at):
        chunk = lax.rem(z + at // PIECES + 1, rows)
        ref = part(chunk, PIECES - 1 - lax.rem(at, PIECES))
        return send(ref, ref, dn_s.at[0], dn_r.at[at % TAKES], (z_dn, y, d))

    def start_dn():
        admitted(dn)
        for i in range(PIECES):
            dn_copy(i).start()

    outer = jnp.logical_or(z == 0, z == rows - 1)

    @pl.when(jnp.logical_not(outer))
    def _():
        start_dn()

    admitted(up)
    for i in range(PIECES):
        up_copy(i).start()

    @pl.when(z == rows - 1)
    def _():
        start_dn()

    share = height // 2
    mine = core * share
    to_right, to_left, to_twin = (z, y_up, d), (z, y_dn, d), (z, y, twin)

    def near_copies():
        ref = left_rows(y, mine, share)
        return (
            send(ref, ref, left_s.at[0], left_r.at[0], to_right),
            send(ref, ref, left_s.at[0], left_r.at[0], to_left),
        )

    def far_copies():
        a = left_rows(y_dn, mine, share // 2)
        b = left_rows(y_up, mine + share // 2, share // 2)
        return (
            send(a, a, left_s.at[0], left_r.at[1], to_right),
            send(b, b, left_s.at[0], left_r.at[1], to_left),
        )

    def twin_copy(col):
        ref = left_rows(col, mine, share)
        return send(ref, ref, left_s.at[1], left_r.at[2], to_twin)

    def all_of(size, which_s, which_r):
        ref = lpan.at[pl.ds(0, size)]
        return send(ref, ref, left_s.at[which_s], left_r.at[which_r], to_twin)

    own_left.wait()
    own_right.wait()
    admitted(right_of)
    admitted(left_of)
    for c in near_copies():
        c.start()
    out[...] = jnp.zeros_like(out)

    @pl.when(z == 0)
    def _():
        start_dn()

    def add_product(chunk):
        col = chunk // per_col
        at = pl.ds(pl.multiple_of(lax.rem(chunk, per_col) * depth, 128), depth)
        out[...] += jnp.dot(
            left_rows(col)[:, at], chunk_rows(chunk)[...], preferred_element_type=jnp.float32
        )

    total = (rows - 1) * PIECES

    def below(at):
        count = total // 2
        for plane, pieces in FROM_BELOW.items():
            count = jnp.where(at == plane, jnp.where(core == 0, *pieces), count)
        return count

    mine_up, mine_dn = below(z), total - below(z)
    next_up, next_dn = below(z_up), total - below(z_dn)
    lag = 0
    for plane, pieces in LAG.items():
        lag = jnp.where(z == plane, pieces, lag)

    def all_sent(count, sem, counts):
        for n in sorted(counts):
            ref = rpan.at[pl.ds(0, n * piece)]

            @pl.when(count == n)
            def _():
                send(ref, ref, sem.at[0], up_r.at[0], (z_up, y, d)).wait_send()

    seven = half_steps - 1
    regular = 2 * seven
    blocks = depth // BLOCK
    swapped = mine_up < seven * PIECES

    def piece_at(distance, i):
        at = (distance - 1) * PIECES + i
        other = (rows - distance - 1) * PIECES + PIECES - 1 - i
        return jnp.where(at < mine_up, at + lag, other)

    def block_at(distance, n):
        first, last = n * BLOCK // piece, ((n + 1) * BLOCK - 1) // piece
        return functools.reduce(
            jnp.maximum, [piece_at(distance, i) for i in range(first, last + 1)]
        )

    ready = []
    for n in range(blocks):
        low, high = block_at(seven, n), block_at(half_steps, blocks - 1 - n)
        if n == blocks - 1:
            low, high = jnp.where(swapped, high, low), jnp.where(swapped, low, high)
        ready += [low, high]
    for n in range(1, len(ready)):
        ready[n] = jnp.maximum(ready[n], ready[n - 1])

    def entry_chunk(e):
        distance = (e + 1) // 2
        sign = 2 * lax.rem(e, 2) - 1
        return lax.rem(z + sign * distance + rows, rows)

    def add_block(e):
        e = jnp.where(jnp.logical_and(swapped, e >= 2 * blocks - 2), 4 * blocks - 3 - e, e)
        upper = lax.rem(e, 2)
        chunk = lax.rem(z + half_steps + 1 - upper, rows)
        n = jnp.where(upper == 1, blocks - 1 - e // 2, e // 2)
        col = chunk // per_col
        at = lax.rem(chunk, per_col) * depth + n * BLOCK
        out[...] += jnp.dot(
            left_rows(col)[:, pl.ds(pl.multiple_of(at, 128), BLOCK)],
            chunk_rows(chunk, n * BLOCK, BLOCK)[...],
            preferred_element_type=jnp.float32,
        )

    def whole_after(at):
        from_above = jnp.minimum((at + 1) // PIECES, seven)
        from_below = jnp.clip((at + 1 - lag) // PIECES, 0, seven - 1)
        count = 2 * from_below + jnp.where(from_above > from_below, 2, 1)
        more = sum(jnp.where(at >= r, 1, 0) for r in ready)
        return count + jnp.where(count == regular, more, 0)

    turns = jnp.maximum(mine_up + lag, mine_dn)

    def take(at, done):
        at_up = at - lag

        @pl.when(jnp.logical_and(at_up >= 0, at_up < mine_up))
        def _():
            up_arrival(at_up).wait_recv()

            @pl.when(at_up + PIECES < next_up)
            def _():
                up_copy(at_up + PIECES).start()

        @pl.when(at < mine_dn)
        def _():
            dn_arrival(at).wait_recv()

            @pl.when(at + PIECES < next_dn)
            def _():
                dn_copy(at + PIECES).start()

        @pl.when(at == LEFT_NEAR * PIECES)
        def _():
            all_of(2 * share, 0, 0).wait_recv()
            for c in far_copies():
                c.start()
            admitted(beside)
            twin_copy(y_dn).start()
            twin_copy(y_up).start()

        @pl.when(at == LEFT_FAR * PIECES)
        def _():
            all_of(share, 0, 1).wait_recv()
            twin_copy(y_far).start()

        @pl.when(at == LEFT_READY * PIECES)
        def _():
            all_of(3 * share, 1, 2).wait_recv()
            all_of(3 * share, 0, 0).wait_send()
            all_of(3 * share, 1, 0).wait_send()

        whole = jnp.where(at < LEFT_READY * PIECES, 0, whole_after(at))
        upto = jnp.where(at == turns - 1, whole, jnp.minimum(whole, done + PER_TURN))

        def body(e, c):
            @pl.when(e < regular)
            def _():
                add_product(entry_chunk(e))

            @pl.when(e >= regular)
            def _():
                add_block(e - regular)

            return c

        lax.fori_loop(done, upto, body, 0)
        return upto

    lax.fori_loop(0, turns, take, 0)
    counts = {total // 2}.union(*FROM_BELOW.values())
    all_sent(next_up, up_s, counts)
    all_sent(next_dn, dn_s, {total - n for n in counts})


def on_device(left_block, right_block):
    rows, cols = lax.axis_size("row"), lax.axis_size("col")
    layers = lax.axis_size("depth")
    height, left_cols = left_block.shape
    depth, right_cols = right_block.shape
    width = right_cols // layers
    dma = pltpu.SemaphoreType.DMA
    return pl.pallas_call(
        kernel,
        out_shape=pltpu.VMEM((height, width), jnp.float32),
        in_specs=[pl.BlockSpec(memory_space=pl.ANY)] * 2,
        out_specs=pl.BlockSpec(memory_space=pltpu.VMEM),
        scratch_shapes=[
            pltpu.VMEM((cols * height, left_cols), jnp.bfloat16),
            pltpu.VMEM((rows * depth, width), jnp.bfloat16),
            pltpu.SemaphoreType.REGULAR((5,)),
            dma((2,)),
            dma((1,)),
            dma((TAKES,)),
            dma((1,)),
            dma((TAKES,)),
            dma((2,)),
            dma((3,)),
        ],
        compiler_params=pltpu.CompilerParams(
            collective_id=0, has_side_effects=True, vmem_limit_bytes=63 << 20
        ),
        cost_estimate=pl.CostEstimate(
            flops=2 * height * width * depth * rows,
            bytes_accessed=2 * height * left_cols + 2 * depth * width + 4 * height * width,
            transcendentals=0,
        ),
    )(left_block, right_block)


def solution(mesh):
    return jax.shard_map(
        on_device,
        mesh=mesh,
        in_specs=(P("row", "col"), P("row", "col")),
        out_specs=P("row", ("col", "depth")),
        check_vma=False,
    )
```

```python
import functools

import jax
import jax.numpy as jnp
from jax import lax
from jax.experimental import pallas as pl
from jax.experimental.pallas import tpu as pltpu
from jax.sharding import PartitionSpec as P

PIECES = 4
TAKES = 3 * PIECES + 1
FROM_BELOW = {0: (27, 28), 1: (28, 28), 15: (32, 32)}
LAG = {0: 4, 1: 3, 2: 2, 3: 1}
LEFT_NEAR = 3
LEFT_FAR = 4
LEFT_READY = 5
PER_TURN = 2


def kernel(
    left, right, out, lpan, rpan,
    answer, own_sem, up_s, up_r, dn_s, dn_r, left_s, left_r,
):
    rows = lax.axis_size("row")
    cols = lax.axis_size("col")
    z, y, d = lax.axis_index("row"), lax.axis_index("col"), lax.axis_index("depth")
    depth, width = right.shape[0], rpan.shape[1]
    height = left.shape[0]
    half_steps = rows // 2
    piece = depth // PIECES
    per_col = left.shape[1] // depth

    z_up, z_dn = lax.rem(z + 1, rows), lax.rem(z + rows - 1, rows)
    y_up, y_dn = lax.rem(y + 1, cols), lax.rem(y + cols - 1, cols)
    y_far = lax.rem(y + 2, cols)
    core = lax.rem(d, 2)
    twin = d + 1 - 2 * core

    def chunk_rows(chunk, first=0, size=depth):
        return rpan.at[pl.ds(pl.multiple_of(chunk * depth + first, 16), size)]

    def left_rows(col, first=0, size=height):
        return lpan.at[pl.ds(pl.multiple_of(col * height + first, 16), size)]

    my_cols = pl.ds(pl.multiple_of(d * width, 128), width)
    own_right = pltpu.make_async_copy(right.at[:, my_cols], chunk_rows(z), own_sem.at[1])
    own_left = pltpu.make_async_copy(left, left_rows(y), own_sem.at[0])

    turned = jnp.logical_and(z == 0, d == 0)
    up, dn, right_of, left_of, beside = range(5)
    peers = ((z_up, y, d), (z_dn, y, d), (z, y_up, d), (z, y_dn, d), (z, y, twin))
    greets = (
        z < rows - 2,
        jnp.logical_or(z == 0, z == rows - 1),
        jnp.logical_xor(y != cols - 1, turned),
        jnp.logical_xor(y == 0, turned),
        core == 1,
    )
    back = (dn, up, left_of, right_of, beside)

    barrier = pltpu.get_barrier_semaphore()
    greeted = 0
    for who, first in zip(peers, greets):
        greeted = greeted + jnp.where(first, 0, 1)

        @pl.when(first)
        def _():
            pl.semaphore_signal(barrier, inc=1, device_id=who)

    @pl.when(greeted > 0)
    def _():
        pl.semaphore_wait(barrier, greeted)

    for side, (who, first) in enumerate(zip(peers, greets)):
        @pl.when(jnp.logical_not(first))
        def _():
            pl.semaphore_signal(answer.at[back[side]], inc=1, device_id=who)

    def admitted(side):
        @pl.when(greets[side])
        def _():
            pl.semaphore_wait(answer.at[side], 1)

    def part(chunk, i):
        return chunk_rows(chunk, i * piece, piece)

    def send(src, dst, send_sem, recv_sem, who):
        return pltpu.make_async_remote_copy(
            src_ref=src, dst_ref=dst, send_sem=send_sem, recv_sem=recv_sem,
            device_id=who,
        )

    def up_copy(at):
        chunk = lax.rem(z - at // PIECES + rows, rows)
        ref = part(chunk, lax.rem(at, PIECES))
        src = right.at[pl.ds(at * piece, piece), my_cols] if isinstance(at, int) else ref
        return send(src, ref, up_s.at[0], up_r.at[at % TAKES], (z_up, y, d))

    def dn_copy(at):
        chunk = lax.rem(z + at // PIECES, rows)
        ref = part(chunk, PIECES - 1 - lax.rem(at, PIECES))
        src = right.at[pl.ds((PIECES - 1 - at) * piece, piece), my_cols] if isinstance(at, int) else ref
        return send(src, ref, dn_s.at[0], dn_r.at[at % TAKES], (z_dn, y, d))

    def up_arrival(at):
        chunk = lax.rem(z - at // PIECES - 1 + rows, rows)
        ref = part(chunk, lax.rem(at, PIECES))
        return send(ref, ref, up_s.at[0], up_r.at[at % TAKES], (z_up, y, d))

    def dn_arrival(at):
        chunk = lax.rem(z + at // PIECES + 1, rows)
        ref = part(chunk, PIECES - 1 - lax.rem(at, PIECES))
        return send(ref, ref, dn_s.at[0], dn_r.at[at % TAKES], (z_dn, y, d))

    def start_dn():
        admitted(dn)
        for i in range(PIECES):
            dn_copy(i).start()

    outer = jnp.logical_or(z == 0, z == rows - 1)

    @pl.when(jnp.logical_not(outer))
    def _():
        start_dn()

    admitted(up)
    for i in range(PIECES):
        up_copy(i).start()

    @pl.when(z == rows - 1)
    def _():
        start_dn()

    own_left.start()
    own_right.start()

    share = height // 2
    mine = core * share
    to_right, to_left, to_twin = (z, y_up, d), (z, y_dn, d), (z, y, twin)

    def near_copies():
        ref = left_rows(y, mine, share)
        src = left.at[pl.ds(pl.multiple_of(mine, 16), share)]
        return (
            send(src, ref, left_s.at[0], left_r.at[0], to_right),
            send(src, ref, left_s.at[0], left_r.at[0], to_left),
        )

    def far_copies():
        a = left_rows(y_dn, mine, share // 2)
        b = left_rows(y_up, mine + share // 2, share // 2)
        return (
            send(a, a, left_s.at[0], left_r.at[1], to_right),
            send(b, b, left_s.at[0], left_r.at[1], to_left),
        )

    def twin_copy(col):
        ref = left_rows(col, mine, share)
        return send(ref, ref, left_s.at[1], left_r.at[2], to_twin)

    def all_of(size, which_s, which_r):
        ref = lpan.at[pl.ds(0, size)]
        return send(ref, ref, left_s.at[which_s], left_r.at[which_r], to_twin)

    admitted(right_of)
    admitted(left_of)
    for c in near_copies():
        c.start()
    out[...] = jnp.zeros_like(out)

    @pl.when(z == 0)
    def _():
        start_dn()

    def add_product(chunk):
        col = chunk // per_col
        at = pl.ds(pl.multiple_of(lax.rem(chunk, per_col) * depth, 128), depth)
        out[...] += jnp.dot(
            left_rows(col)[:, at], chunk_rows(chunk)[...], preferred_element_type=jnp.float32
        )

    total = (rows - 1) * PIECES

    def below(at):
        count = total // 2
        for plane, pieces in FROM_BELOW.items():
            count = jnp.where(at == plane, jnp.where(core == 0, *pieces), count)
        return count

    mine_up, mine_dn = below(z), total - below(z)
    next_up, next_dn = below(z_up), total - below(z_dn)
    lag = 0
    for plane, pieces in LAG.items():
        lag = jnp.where(z == plane, pieces, lag)

    def all_sent(count, sem, counts):
        for n in sorted(counts):
            ref = rpan.at[pl.ds(0, n * piece)]

            @pl.when(count == n)
            def _():
                send(ref, ref, sem.at[0], up_r.at[0], (z_up, y, d)).wait_send()

    seven = half_steps - 1
    whole_7 = jnp.where(mine_up >= seven * PIECES, seven * PIECES - 1 + lag, mine_dn - 1)
    whole_8 = jnp.where(
        mine_dn >= half_steps * PIECES,
        half_steps * PIECES - 1,
        jnp.maximum(mine_up - 1 + lag, mine_dn - 1),
    )
    turn_round = whole_8 < whole_7
    whole_first = jnp.minimum(whole_7, whole_8)
    whole_second = jnp.maximum(whole_7, whole_8)
    regular = 2 * seven

    def entry_chunk(e):
        e = jnp.where(jnp.logical_and(turn_round, e >= regular), 2 * regular + 1 - e, e)
        distance = (e + 1) // 2
        sign = 2 * lax.rem(e, 2) - 1
        return lax.rem(z + sign * distance + rows, rows)

    def whole_after(at):
        from_above = jnp.minimum((at + 1) // PIECES, seven)
        from_below = jnp.clip((at + 1 - lag) // PIECES, 0, seven - 1)
        count = 2 * from_below + jnp.where(from_above > from_below, 2, 1)
        more = jnp.where(at >= whole_first, 1, 0) + jnp.where(at >= whole_second, 1, 0)
        return count + jnp.where(count == regular, more, 0)

    turns = jnp.maximum(mine_up + lag, mine_dn)

    counts = {total // 2}.union(*FROM_BELOW.values())

    def take(at, done):
        at_up = at - lag

        @pl.when(at == turns - 1)
        def _():
            all_sent(next_up, up_s, counts)
            all_sent(next_dn, dn_s, {total - n for n in counts})

        @pl.when(jnp.logical_and(at_up >= 0, at_up < mine_up))
        def _():
            up_arrival(at_up).wait_recv()

            @pl.when(at_up + PIECES < next_up)
            def _():
                up_copy(at_up + PIECES).start()

        @pl.when(at < mine_dn)
        def _():
            dn_arrival(at).wait_recv()

            @pl.when(at + PIECES < next_dn)
            def _():
                dn_copy(at + PIECES).start()

        @pl.when(at == LEFT_NEAR * PIECES)
        def _():
            all_of(2 * share, 0, 0).wait_recv()
            for c in far_copies():
                c.start()
            admitted(beside)
            twin_copy(y_dn).start()
            twin_copy(y_up).start()

        @pl.when(at == LEFT_FAR * PIECES)
        def _():
            all_of(share, 0, 1).wait_recv()
            twin_copy(y_far).start()

        @pl.when(at == LEFT_READY * PIECES)
        def _():
            own_left.wait()
            own_right.wait()
            all_of(3 * share, 1, 2).wait_recv()
            all_of(3 * share, 0, 0).wait_send()
            all_of(3 * share, 1, 0).wait_send()

        whole = jnp.where(at < LEFT_READY * PIECES, 0, whole_after(at))
        upto = jnp.where(at == turns - 1, whole, jnp.minimum(whole, done + PER_TURN))

        def body(e, c):
            add_product(entry_chunk(e))
            return c

        lax.fori_loop(done, upto, body, 0)
        return upto

    lax.fori_loop(0, turns, take, 0)


def on_device(left_block, right_block):
    rows, cols = lax.axis_size("row"), lax.axis_size("col")
    layers = lax.axis_size("depth")
    height, left_cols = left_block.shape
    depth, right_cols = right_block.shape
    width = right_cols // layers
    dma = pltpu.SemaphoreType.DMA
    return pl.pallas_call(
        kernel,
        out_shape=pltpu.VMEM((height, width), jnp.float32),
        in_specs=[pl.BlockSpec(memory_space=pl.ANY)] * 2,
        out_specs=pl.BlockSpec(memory_space=pltpu.VMEM),
        scratch_shapes=[
            pltpu.VMEM((cols * height, left_cols), jnp.bfloat16),
            pltpu.VMEM((rows * depth, width), jnp.bfloat16),
            pltpu.SemaphoreType.REGULAR((5,)),
            dma((2,)),
            dma((1,)),
            dma((TAKES,)),
            dma((1,)),
            dma((TAKES,)),
            dma((2,)),
            dma((3,)),
        ],
        compiler_params=pltpu.CompilerParams(
            collective_id=0, has_side_effects=True, vmem_limit_bytes=63 << 20
        ),
        cost_estimate=pl.CostEstimate(
            flops=2 * height * width * depth * rows,
            bytes_accessed=2 * height * left_cols + 2 * depth * width + 4 * height * width,
            transcendentals=0,
        ),
    )(left_block, right_block)


def solution(mesh):
    return jax.shard_map(
        on_device,
        mesh=mesh,
        in_specs=(P("row", "col"), P("row", "col")),
        out_specs=P("row", ("col", "depth")),
        check_vma=False,
    )
```

```python
import functools

import jax
import jax.numpy as jnp
from jax import lax
from jax.experimental import pallas as pl
from jax.experimental.pallas import tpu as pltpu
from jax.sharding import PartitionSpec as P

PIECES = 4
TAKES = 3 * PIECES + 1
FROM_BELOW = {0: (27, 28), 1: (28, 29), 15: (32, 32)}
LAG = {0: (4, 4), 1: (3, 2), 2: (2, 1), 3: (1, 1)}
LEFT_NEAR = 3
LEFT_FAR = 4
LEFT_READY = 5
PER_TURN = 2


def kernel(
    left, right, out, lpan, rpan,
    answer, own_sem, up_s, up_r, dn_s, dn_r, left_s, left_r,
):
    rows = lax.axis_size("row")
    cols = lax.axis_size("col")
    z, y, d = lax.axis_index("row"), lax.axis_index("col"), lax.axis_index("depth")
    depth, width = right.shape[0], rpan.shape[1]
    height = left.shape[0]
    half_steps = rows // 2
    piece = depth // PIECES
    per_col = left.shape[1] // depth

    z_up, z_dn = lax.rem(z + 1, rows), lax.rem(z + rows - 1, rows)
    y_up, y_dn = lax.rem(y + 1, cols), lax.rem(y + cols - 1, cols)
    y_far = lax.rem(y + 2, cols)
    core = lax.rem(d, 2)
    twin = d + 1 - 2 * core

    def chunk_rows(chunk, first=0, size=depth):
        return rpan.at[pl.ds(pl.multiple_of(chunk * depth + first, 16), size)]

    def left_rows(col, first=0, size=height):
        return lpan.at[pl.ds(pl.multiple_of(col * height + first, 16), size)]

    my_cols = pl.ds(pl.multiple_of(d * width, 128), width)
    own_right = pltpu.make_async_copy(right.at[:, my_cols], chunk_rows(z), own_sem.at[1])
    own_left = pltpu.make_async_copy(left, left_rows(y), own_sem.at[0])

    turned = jnp.logical_and(z == 0, d == 0)
    up, dn, right_of, left_of, beside = range(5)
    peers = ((z_up, y, d), (z_dn, y, d), (z, y_up, d), (z, y_dn, d), (z, y, twin))
    greets = (
        z < rows - 2,
        jnp.logical_or(z == 0, z == rows - 1),
        jnp.logical_xor(y != cols - 1, turned),
        jnp.logical_xor(y == 0, turned),
        core == 1,
    )
    back = (dn, up, left_of, right_of, beside)

    barrier = pltpu.get_barrier_semaphore()
    greeted = 0
    for who, first in zip(peers, greets):
        greeted = greeted + jnp.where(first, 0, 1)

        @pl.when(first)
        def _():
            pl.semaphore_signal(barrier, inc=1, device_id=who)

    @pl.when(greeted > 0)
    def _():
        pl.semaphore_wait(barrier, greeted)

    for side, (who, first) in enumerate(zip(peers, greets)):
        @pl.when(jnp.logical_not(first))
        def _():
            pl.semaphore_signal(answer.at[back[side]], inc=1, device_id=who)

    def admitted(side):
        @pl.when(greets[side])
        def _():
            pl.semaphore_wait(answer.at[side], 1)

    def part(chunk, i):
        return chunk_rows(chunk, i * piece, piece)

    def send(src, dst, send_sem, recv_sem, who):
        return pltpu.make_async_remote_copy(
            src_ref=src, dst_ref=dst, send_sem=send_sem, recv_sem=recv_sem,
            device_id=who,
        )

    def up_copy(at):
        chunk = lax.rem(z - at // PIECES + rows, rows)
        ref = part(chunk, lax.rem(at, PIECES))
        src = right.at[pl.ds(at * piece, piece), my_cols] if isinstance(at, int) else ref
        return send(src, ref, up_s.at[0], up_r.at[at % TAKES], (z_up, y, d))

    def dn_copy(at):
        chunk = lax.rem(z + at // PIECES, rows)
        ref = part(chunk, PIECES - 1 - lax.rem(at, PIECES))
        src = right.at[pl.ds((PIECES - 1 - at) * piece, piece), my_cols] if isinstance(at, int) else ref
        return send(src, ref, dn_s.at[0], dn_r.at[at % TAKES], (z_dn, y, d))

    def up_arrival(at):
        chunk = lax.rem(z - at // PIECES - 1 + rows, rows)
        ref = part(chunk, lax.rem(at, PIECES))
        return send(ref, ref, up_s.at[0], up_r.at[at % TAKES], (z_up, y, d))

    def dn_arrival(at):
        chunk = lax.rem(z + at // PIECES + 1, rows)
        ref = part(chunk, PIECES - 1 - lax.rem(at, PIECES))
        return send(ref, ref, dn_s.at[0], dn_r.at[at % TAKES], (z_dn, y, d))

    def start_dn():
        admitted(dn)
        for i in range(PIECES):
            dn_copy(i).start()

    outer = jnp.logical_or(z == 0, z == rows - 1)

    @pl.when(jnp.logical_not(outer))
    def _():
        start_dn()

    admitted(up)
    for i in range(PIECES):
        up_copy(i).start()

    @pl.when(z == rows - 1)
    def _():
        start_dn()

    own_left.start()
    own_right.start()

    share = height // 2
    mine = core * share
    to_right, to_left, to_twin = (z, y_up, d), (z, y_dn, d), (z, y, twin)

    def near_copies():
        ref = left_rows(y, mine, share)
        src = left.at[pl.ds(pl.multiple_of(mine, 16), share)]
        return (
            send(src, ref, left_s.at[0], left_r.at[0], to_right),
            send(src, ref, left_s.at[0], left_r.at[0], to_left),
        )

    def far_copies():
        a = left_rows(y_dn, mine, share // 2)
        b = left_rows(y_up, mine + share // 2, share // 2)
        return (
            send(a, a, left_s.at[0], left_r.at[1], to_right),
            send(b, b, left_s.at[0], left_r.at[1], to_left),
        )

    def twin_copy(col):
        ref = left_rows(col, mine, share)
        return send(ref, ref, left_s.at[1], left_r.at[2], to_twin)

    def all_of(size, which_s, which_r):
        ref = lpan.at[pl.ds(0, size)]
        return send(ref, ref, left_s.at[which_s], left_r.at[which_r], to_twin)

    admitted(right_of)
    admitted(left_of)
    for c in near_copies():
        c.start()
    out[...] = jnp.zeros_like(out)

    @pl.when(z == 0)
    def _():
        start_dn()

    def add_product(chunk):
        col = chunk // per_col
        at = pl.ds(pl.multiple_of(lax.rem(chunk, per_col) * depth, 128), depth)
        out[...] += jnp.dot(
            left_rows(col)[:, at], chunk_rows(chunk)[...], preferred_element_type=jnp.float32
        )

    total = (rows - 1) * PIECES

    def below(at):
        count = total // 2
        for plane, pieces in FROM_BELOW.items():
            count = jnp.where(at == plane, jnp.where(core == 0, *pieces), count)
        return count

    mine_up, mine_dn = below(z), total - below(z)
    next_up, next_dn = below(z_up), total - below(z_dn)
    lag = 0
    for plane, pieces in LAG.items():
        lag = jnp.where(z == plane, jnp.where(core == 0, *pieces), lag)

    def all_sent(count, sem, counts):
        for n in sorted(counts):
            ref = rpan.at[pl.ds(0, n * piece)]

            @pl.when(count == n)
            def _():
                send(ref, ref, sem.at[0], up_r.at[0], (z_up, y, d)).wait_send()

    seven = half_steps - 1
    whole_7 = jnp.where(mine_up >= seven * PIECES, seven * PIECES - 1 + lag, mine_dn - 1)
    whole_8 = jnp.where(
        mine_dn >= half_steps * PIECES,
        half_steps * PIECES - 1,
        jnp.maximum(mine_up - 1 + lag, mine_dn - 1),
    )
    turn_round = whole_8 < whole_7
    whole_first = jnp.minimum(whole_7, whole_8)
    whole_second = jnp.maximum(whole_7, whole_8)
    regular = 2 * seven

    def entry_chunk(e):
        e = jnp.where(jnp.logical_and(turn_round, e >= regular), 2 * regular + 1 - e, e)
        distance = (e + 1) // 2
        sign = 2 * lax.rem(e, 2) - 1
        return lax.rem(z + sign * distance + rows, rows)

    def whole_after(at):
        from_above = jnp.minimum((at + 1) // PIECES, seven)
        from_below = jnp.clip((at + 1 - lag) // PIECES, 0, seven - 1)
        count = 2 * from_below + jnp.where(from_above > from_below, 2, 1)
        more = jnp.where(at >= whole_first, 1, 0) + jnp.where(at >= whole_second, 1, 0)
        return count + jnp.where(count == regular, more, 0)

    turns = jnp.maximum(mine_up + lag, mine_dn)

    def take(at, done):
        at_up = at - lag

        @pl.when(jnp.logical_and(at_up >= 0, at_up < mine_up))
        def _():
            up_arrival(at_up).wait_recv()

            @pl.when(at_up + PIECES < next_up)
            def _():
                up_copy(at_up + PIECES).start()

        @pl.when(at < mine_dn)
        def _():
            dn_arrival(at).wait_recv()

            @pl.when(at + PIECES < next_dn)
            def _():
                dn_copy(at + PIECES).start()

        @pl.when(at == LEFT_NEAR * PIECES)
        def _():
            all_of(2 * share, 0, 0).wait_recv()
            for c in far_copies():
                c.start()
            admitted(beside)
            twin_copy(y_dn).start()
            twin_copy(y_up).start()

        @pl.when(at == LEFT_FAR * PIECES)
        def _():
            all_of(share, 0, 1).wait_recv()
            twin_copy(y_far).start()

        @pl.when(at == LEFT_READY * PIECES)
        def _():
            own_left.wait()
            own_right.wait()
            all_of(3 * share, 1, 2).wait_recv()
            all_of(3 * share, 0, 0).wait_send()
            all_of(3 * share, 1, 0).wait_send()

        whole = jnp.where(at < LEFT_READY * PIECES, 0, whole_after(at))
        upto = jnp.where(at == turns - 1, whole, jnp.minimum(whole, done + PER_TURN))

        def body(e, c):
            add_product(entry_chunk(e))
            return c

        lax.fori_loop(done, upto, body, 0)
        return upto

    lax.fori_loop(0, turns, take, 0)
    counts = {total // 2}.union(*FROM_BELOW.values())
    all_sent(next_up, up_s, counts)
    all_sent(next_dn, dn_s, {total - n for n in counts})


def on_device(left_block, right_block):
    rows, cols = lax.axis_size("row"), lax.axis_size("col")
    layers = lax.axis_size("depth")
    height, left_cols = left_block.shape
    depth, right_cols = right_block.shape
    width = right_cols // layers
    dma = pltpu.SemaphoreType.DMA
    return pl.pallas_call(
        kernel,
        out_shape=pltpu.VMEM((height, width), jnp.float32),
        in_specs=[pl.BlockSpec(memory_space=pl.ANY)] * 2,
        out_specs=pl.BlockSpec(memory_space=pltpu.VMEM),
        scratch_shapes=[
            pltpu.VMEM((cols * height, left_cols), jnp.bfloat16),
            pltpu.VMEM((rows * depth, width), jnp.bfloat16),
            pltpu.SemaphoreType.REGULAR((5,)),
            dma((2,)),
            dma((1,)),
            dma((TAKES,)),
            dma((1,)),
            dma((TAKES,)),
            dma((2,)),
            dma((3,)),
        ],
        compiler_params=pltpu.CompilerParams(
            collective_id=0, has_side_effects=True, vmem_limit_bytes=63 << 20
        ),
        cost_estimate=pl.CostEstimate(
            flops=2 * height * width * depth * rows,
            bytes_accessed=2 * height * left_cols + 2 * depth * width + 4 * height * width,
            transcendentals=0,
        ),
    )(left_block, right_block)


def solution(mesh):
    return jax.shard_map(
        on_device,
        mesh=mesh,
        in_specs=(P("row", "col"), P("row", "col")),
        out_specs=P("row", ("col", "depth")),
        check_vma=False,
    )
```

```python
import functools

import jax
import jax.numpy as jnp
from jax import lax
from jax.experimental import pallas as pl
from jax.experimental.pallas import tpu as pltpu
from jax.sharding import PartitionSpec as P

PIECES = 4
TAKES = 3 * PIECES + 1
FROM_BELOW = {0: (27, 28), 1: (28, 28), 15: (32, 32)}
LAG = {0: 4, 1: 3, 2: 2, 3: 1}
LEFT_NEAR = 2
LEFT_FAR = 3
LEFT_READY = 4
PER_TURN = 2


def kernel(
    left, right, out, lpan, rpan,
    answer, own_sem, up_s, up_r, dn_s, dn_r, left_s, left_r,
):
    rows = lax.axis_size("row")
    cols = lax.axis_size("col")
    z, y, d = lax.axis_index("row"), lax.axis_index("col"), lax.axis_index("depth")
    depth, width = right.shape[0], rpan.shape[1]
    height = left.shape[0]
    half_steps = rows // 2
    piece = depth // PIECES
    per_col = left.shape[1] // depth

    z_up, z_dn = lax.rem(z + 1, rows), lax.rem(z + rows - 1, rows)
    y_up, y_dn = lax.rem(y + 1, cols), lax.rem(y + cols - 1, cols)
    y_far = lax.rem(y + 2, cols)
    core = lax.rem(d, 2)
    twin = d + 1 - 2 * core

    def chunk_rows(chunk, first=0, size=depth):
        return rpan.at[pl.ds(pl.multiple_of(chunk * depth + first, 16), size)]

    def left_rows(col, first=0, size=height):
        return lpan.at[pl.ds(pl.multiple_of(col * height + first, 16), size)]

    my_cols = pl.ds(pl.multiple_of(d * width, 128), width)
    own_right = pltpu.make_async_copy(right.at[:, my_cols], chunk_rows(z), own_sem.at[1])
    own_left = pltpu.make_async_copy(left, left_rows(y), own_sem.at[0])
    own_right.start()
    own_left.start()

    turned = jnp.logical_and(z == 0, d == 0)
    up, dn, right_of, left_of, beside = range(5)
    peers = ((z_up, y, d), (z_dn, y, d), (z, y_up, d), (z, y_dn, d), (z, y, twin))
    greets = (
        z < rows - 2,
        jnp.logical_or(z == 0, z == rows - 1),
        jnp.logical_xor(y != cols - 1, turned),
        jnp.logical_xor(y == 0, turned),
        core == 1,
    )
    back = (dn, up, left_of, right_of, beside)

    barrier = pltpu.get_barrier_semaphore()
    greeted = 0
    for who, first in zip(peers, greets):
        greeted = greeted + jnp.where(first, 0, 1)

        @pl.when(first)
        def _():
            pl.semaphore_signal(barrier, inc=1, device_id=who)

    @pl.when(greeted > 0)
    def _():
        pl.semaphore_wait(barrier, greeted)

    for side, (who, first) in enumerate(zip(peers, greets)):
        @pl.when(jnp.logical_not(first))
        def _():
            pl.semaphore_signal(answer.at[back[side]], inc=1, device_id=who)

    def admitted(side):
        @pl.when(greets[side])
        def _():
            pl.semaphore_wait(answer.at[side], 1)

    def part(chunk, i):
        return chunk_rows(chunk, i * piece, piece)

    def send(src, dst, send_sem, recv_sem, who):
        return pltpu.make_async_remote_copy(
            src_ref=src, dst_ref=dst, send_sem=send_sem, recv_sem=recv_sem,
            device_id=who,
        )

    def up_copy(at):
        chunk = lax.rem(z - at // PIECES + rows, rows)
        ref = part(chunk, lax.rem(at, PIECES))
        src = right.at[pl.ds(at * piece, piece), my_cols] if isinstance(at, int) else ref
        return send(src, ref, up_s.at[0], up_r.at[at % TAKES], (z_up, y, d))

    def dn_copy(at):
        chunk = lax.rem(z + at // PIECES, rows)
        ref = part(chunk, PIECES - 1 - lax.rem(at, PIECES))
        src = right.at[pl.ds((PIECES - 1 - at) * piece, piece), my_cols] if isinstance(at, int) else ref
        return send(src, ref, dn_s.at[0], dn_r.at[at % TAKES], (z_dn, y, d))

    def up_arrival(at):
        chunk = lax.rem(z - at // PIECES - 1 + rows, rows)
        ref = part(chunk, lax.rem(at, PIECES))
        return send(ref, ref, up_s.at[0], up_r.at[at % TAKES], (z_up, y, d))

    def dn_arrival(at):
        chunk = lax.rem(z + at // PIECES + 1, rows)
        ref = part(chunk, PIECES - 1 - lax.rem(at, PIECES))
        return send(ref, ref, dn_s.at[0], dn_r.at[at % TAKES], (z_dn, y, d))

    def start_dn():
        admitted(dn)
        for i in range(PIECES):
            dn_copy(i).start()

    outer = jnp.logical_or(z == 0, z == rows - 1)

    @pl.when(jnp.logical_not(outer))
    def _():
        start_dn()

    admitted(up)
    for i in range(PIECES):
        up_copy(i).start()

    @pl.when(z == rows - 1)
    def _():
        start_dn()

    share = height // 2
    mine = core * share
    to_right, to_left, to_twin = (z, y_up, d), (z, y_dn, d), (z, y, twin)

    def near_copies():
        ref = left_rows(y, mine, share)
        return (
            send(ref, ref, left_s.at[0], left_r.at[0], to_right),
            send(ref, ref, left_s.at[0], left_r.at[0], to_left),
        )

    def far_copies():
        a = left_rows(y_dn, mine, share // 2)
        b = left_rows(y_up, mine + share // 2, share // 2)
        return (
            send(a, a, left_s.at[0], left_r.at[1], to_right),
            send(b, b, left_s.at[0], left_r.at[1], to_left),
        )

    def twin_copy(col):
        ref = left_rows(col, mine, share)
        return send(ref, ref, left_s.at[1], left_r.at[2], to_twin)

    def all_of(size, which_s, which_r):
        ref = lpan.at[pl.ds(0, size)]
        return send(ref, ref, left_s.at[which_s], left_r.at[which_r], to_twin)

    own_left.wait()
    own_right.wait()
    admitted(right_of)
    admitted(left_of)
    for c in near_copies():
        c.start()
    out[...] = jnp.zeros_like(out)

    @pl.when(z == 0)
    def _():
        start_dn()

    def add_product(chunk):
        col = chunk // per_col
        at = pl.ds(pl.multiple_of(lax.rem(chunk, per_col) * depth, 128), depth)
        out[...] += jnp.dot(
            left_rows(col)[:, at], chunk_rows(chunk)[...], preferred_element_type=jnp.float32
        )

    total = (rows - 1) * PIECES

    def below(at):
        count = total // 2
        for plane, pieces in FROM_BELOW.items():
            count = jnp.where(at == plane, jnp.where(core == 0, *pieces), count)
        return count

    mine_up, mine_dn = below(z), total - below(z)
    next_up, next_dn = below(z_up), total - below(z_dn)
    lag = 0
    for plane, pieces in LAG.items():
        lag = jnp.where(z == plane, pieces, lag)

    def all_sent(count, sem, counts):
        for n in sorted(counts):
            ref = rpan.at[pl.ds(0, n * piece)]

            @pl.when(count == n)
            def _():
                send(ref, ref, sem.at[0], up_r.at[0], (z_up, y, d)).wait_send()

    seven = half_steps - 1
    whole_7 = jnp.where(mine_up >= seven * PIECES, seven * PIECES - 1 + lag, mine_dn - 1)
    whole_8 = jnp.where(
        mine_dn >= half_steps * PIECES,
        half_steps * PIECES - 1,
        jnp.maximum(mine_up - 1 + lag, mine_dn - 1),
    )
    turn_round = whole_8 < whole_7
    whole_first = jnp.minimum(whole_7, whole_8)
    whole_second = jnp.maximum(whole_7, whole_8)
    regular = 2 * seven

    def entry_chunk(e):
        e = jnp.where(jnp.logical_and(turn_round, e >= regular), 2 * regular + 1 - e, e)
        distance = (e + 1) // 2
        sign = 2 * lax.rem(e, 2) - 1
        return lax.rem(z + sign * distance + rows, rows)

    def whole_after(at):
        from_above = jnp.minimum((at + 1) // PIECES, seven)
        from_below = jnp.clip((at + 1 - lag) // PIECES, 0, seven - 1)
        count = 2 * from_below + jnp.where(from_above > from_below, 2, 1)
        more = jnp.where(at >= whole_first, 1, 0) + jnp.where(at >= whole_second, 1, 0)
        return count + jnp.where(count == regular, more, 0)

    turns = jnp.maximum(mine_up + lag, mine_dn)

    def take(at, done):
        at_up = at - lag

        @pl.when(jnp.logical_and(at_up >= 0, at_up < mine_up))
        def _():
            up_arrival(at_up).wait_recv()

            @pl.when(at_up + PIECES < next_up)
            def _():
                up_copy(at_up + PIECES).start()

        @pl.when(at < mine_dn)
        def _():
            dn_arrival(at).wait_recv()

            @pl.when(at + PIECES < next_dn)
            def _():
                dn_copy(at + PIECES).start()

        @pl.when(at == LEFT_NEAR * PIECES)
        def _():
            all_of(2 * share, 0, 0).wait_recv()
            for c in far_copies():
                c.start()
            admitted(beside)
            twin_copy(y_dn).start()
            twin_copy(y_up).start()

        @pl.when(at == LEFT_FAR * PIECES)
        def _():
            all_of(share, 0, 1).wait_recv()
            twin_copy(y_far).start()

        @pl.when(at == LEFT_READY * PIECES)
        def _():
            all_of(3 * share, 1, 2).wait_recv()
            all_of(3 * share, 0, 0).wait_send()
            all_of(3 * share, 1, 0).wait_send()

        whole = jnp.where(at < LEFT_READY * PIECES, 0, whole_after(at))
        upto = jnp.where(at == turns - 1, whole, jnp.minimum(whole, done + PER_TURN))

        def body(e, c):
            add_product(entry_chunk(e))
            return c

        lax.fori_loop(done, upto, body, 0)
        return upto

    lax.fori_loop(0, turns, take, 0)
    counts = {total // 2}.union(*FROM_BELOW.values())
    all_sent(next_up, up_s, counts)
    all_sent(next_dn, dn_s, {total - n for n in counts})


def on_device(left_block, right_block):
    rows, cols = lax.axis_size("row"), lax.axis_size("col")
    layers = lax.axis_size("depth")
    height, left_cols = left_block.shape
    depth, right_cols = right_block.shape
    width = right_cols // layers
    dma = pltpu.SemaphoreType.DMA
    return pl.pallas_call(
        kernel,
        out_shape=pltpu.VMEM((height, width), jnp.float32),
        in_specs=[pl.BlockSpec(memory_space=pl.ANY)] * 2,
        out_specs=pl.BlockSpec(memory_space=pltpu.VMEM),
        scratch_shapes=[
            pltpu.VMEM((cols * height, left_cols), jnp.bfloat16),
            pltpu.VMEM((rows * depth, width), jnp.bfloat16),
            pltpu.SemaphoreType.REGULAR((5,)),
            dma((2,)),
            dma((1,)),
            dma((TAKES,)),
            dma((1,)),
            dma((TAKES,)),
            dma((2,)),
            dma((3,)),
        ],
        compiler_params=pltpu.CompilerParams(
            collective_id=0, has_side_effects=True, vmem_limit_bytes=63 << 20
        ),
        cost_estimate=pl.CostEstimate(
            flops=2 * height * width * depth * rows,
            bytes_accessed=2 * height * left_cols + 2 * depth * width + 4 * height * width,
            transcendentals=0,
        ),
    )(left_block, right_block)


def solution(mesh):
    return jax.shard_map(
        on_device,
        mesh=mesh,
        in_specs=(P("row", "col"), P("row", "col")),
        out_specs=P("row", ("col", "depth")),
        check_vma=False,
    )
```
